32 devices in a mesh: box: 8 (over z, x), param: 4 (over y, core).
Axes of the slice: x: 2, y: 2, z: 4, core: 2. Of those that a mesh axis runs over, the one named last changes fastest.
Arguments:
- traces: float32 [8, 4, 512, 256], P('box', 'param'), may hold values from -6 to 6
- owners: int32 [8, 4, 512, 1], P('box', 'param'), may hold values from 0 to 3; in each aligned block of 512 rows (0 to 511, 512 to 1023, ..., all dimensions but the last counted through in order) at most 256 rows name the same one
- counts: int32 [8, 4], P('box', 'param'), may hold values from 128 to 512, as said below
- pair_table: int32 [8, 4, 4, 256], P('box', 'param'), may hold values from 0 to 511
- anterp: float32 [256, 512], replicated, may hold values from -0.375 to 0.375
- interp: float32 [2, 512, 256], replicated, may hold values from -0.25 to 0.25
- phase: float32 [8, 4, 3, 512, 256], P('box', 'param'), may hold values from -3.140625 to 3.140625
Outputs:
- weights_out: float32 [8, 4, 2, 512, 256], P('box', 'param')
The draws below stay inside these ranges and needn't reach their ends.
Inputs may be any that keep to these rules, and one draw needn't show every extreme that they name: `owners`: in the 512 rows of one device no owner is named more than 256 times, a bound that some block reaches. `counts`: some device has all 512 blocks live in every draw.
All inputs are finite; a program needn't handle non-finite values.
Results may differ from the reference program's by a relative error of at most 0.00011.
Values sent between devices are 32-bit elements; how exact they have to be, the bound alone decides.
A program may use at most 64 MiB of HBM per device.

```python
import math
import jax
import jax.numpy as jnp
import numpy as np
from jax import lax

K = 256
TRACE = 256
PAIRS_DEV = 512
BLK_DEV = 512
LEVELS = 3
CAP = 256
N_BOX = 8
N_PARAM = 4


def draw_counts(key, part):
    first_key, second_key = jax.random.split(jax.random.fold_in(key, 17))
    values = jax.random.randint(first_key, (N_BOX * N_PARAM,), BLK_DEV // 4, BLK_DEV + 1)
    chosen = jax.random.randint(second_key, (), 0, N_BOX * N_PARAM)
    values = jnp.where(jnp.arange(N_BOX * N_PARAM) == chosen, BLK_DEV, values)
    return values.reshape(N_BOX, N_PARAM).astype(jnp.int32)


def set_ends(values, rng, smallest, high):
    dims = values.shape
    index_at = [jax.random.randint(jax.random.fold_in(rng, axis), (), 0, dims[axis]) for axis in range(len(dims))]
    values = values.at[tuple(index_at)].set(smallest)
    longest = dims.index(max(dims))
    index_at[longest] = (index_at[longest] + 1) % dims[longest]
    return values.at[tuple(index_at)].set(high)


def shard_levels(stream_key, shape, cuts, smallest, top_value):
    loudness = 1.0
    for position, parts in cuts:
        draws = jax.random.uniform(jax.random.fold_in(jax.random.fold_in(stream_key, 6), position), (parts,), jnp.float32, smallest / len(cuts), top_value / len(cuts))
        loudness = loudness * jnp.repeat(jnp.exp(draws), shape[position] // parts).reshape((-1,) + (1,) * (len(shape) - 1 - position))
    return loudness


def shared_out(stream_key, own, number, rows, amount, top, limit, slope):
    order = jax.random.permutation(stream_key, amount)
    heavy_load, ordinary = portions_of(amount, rows * top, limit, slope, True), portions_of(amount, rows * top, limit, slope, False)
    places = jnp.arange(amount)

    def named(sizes, turn):
        used = int((sizes > 0).sum())
        fixed = max(1, used // 4)
        passed = fixed + (places - fixed + turn * (used - fixed)) % max(1, amount - fixed)
        return jnp.zeros((amount,), jnp.int32).at[order[jnp.where(places < fixed, places, passed)]].set(jnp.asarray(sizes, jnp.int32))

    sizes = jnp.where(number % 4 == 0, named(heavy_load, number // 4), named(ordinary, number - number // 4 - 1))
    mixed = jax.random.permutation(jax.random.fold_in(own, 3), amount)
    giver, receiver = mixed[0:amount // 2 * 2:2], mixed[1:amount // 2 * 2:2]
    margin = jnp.minimum(sizes[giver] - 1, limit - sizes[receiver]) // 2
    margin = jnp.where((giver == order[0]) | (receiver == order[0]) | (sizes[receiver] == 0), 0, jnp.maximum(margin, 0))
    passed = jax.random.randint(jax.random.fold_in(own, 4), (amount // 2,), 0, 1 << 20) % (margin + 1)
    sizes = sizes.at[giver].add(-passed).at[receiver].add(passed)
    items = jnp.searchsorted(jnp.cumsum(sizes), jnp.arange(rows * top), side="right").astype(jnp.int32)
    listing = items.reshape(top, rows).T
    listing = listing[jax.random.permutation(jax.random.fold_in(own, 1), rows)]
    turn = jax.random.randint(jax.random.fold_in(own, 2), (rows, 1), 0, top)
    return jnp.take_along_axis(listing, (jnp.arange(top)[None, :] + turn) % top, axis=1)


def portions_of(number_of, total, limit, slope, full):
    loads = [(1 << 20) // math.isqrt(rank ** slope) + 1 for rank in range(1, number_of + 1)]
    largest = limit if full else min(limit, max(-(-total // number_of), total * loads[0] // sum(loads)))
    least = 1 if total - largest >= number_of - 1 else 0
    holding, rest = [largest] + [least] * (number_of - 1), total - largest - least * (number_of - 1)
    while rest > 0:
        movable = [i for i in range(1, number_of) if holding[i] < largest] or [i for i in range(1, number_of) if holding[i] < limit]
        whole, budget = sum([loads[i] for i in movable]), rest
        for i in movable:
            more = min(limit - holding[i], max(1, budget * loads[i] // whole), rest)
            holding[i] = holding[i] + more
            rest = rest - more
    return np.array(holding)


def gaussian(key, dims, scale, bound, shards=(), kind=jnp.bfloat16):
    array = jax.random.normal(key, dims, jnp.float32) * scale
    if len(shards) > 0:
        array = shard_levels(key, dims, shards, -0.22, 0.18) * array
    return jnp.clip(array, min=-bound, max=bound).astype(kind)


def setup_inputs(seed: int = 0) -> dict:
    key_list = jax.random.split(jax.random.key(seed), 8)
    traces = gaussian(key_list[0], (N_BOX, N_PARAM, BLK_DEV, TRACE), 1.0, 6.0, ((0, 8), (1, 4)), jnp.float32)
    owners_keys = jax.random.split(jax.random.fold_in(key_list[1], 1), N_BOX * N_PARAM * BLK_DEV // BLK_DEV)
    owners_turns = jax.random.permutation(jax.random.fold_in(key_list[1], 3), N_BOX * N_PARAM * BLK_DEV // BLK_DEV)
    owners = jax.vmap(lambda own, number: shared_out(jax.random.fold_in(key_list[1], 2), own, number, BLK_DEV, N_PARAM, 1, CAP, 2))(owners_keys, owners_turns).reshape((N_BOX, N_PARAM, BLK_DEV, 1))
    counts = draw_counts(jax.random.fold_in(key_list[7], 71), 0)
    pair_table = set_ends(jax.random.randint(key_list[3], (N_BOX, N_PARAM, N_PARAM, CAP), 0, PAIRS_DEV), jax.random.fold_in(key_list[3], 1), 0, PAIRS_DEV - 1).astype(jnp.int32)
    anterp = gaussian(key_list[4], (TRACE, 2 * K), TRACE ** -0.5, 0.375, (), jnp.float32)
    interp = gaussian(key_list[5], (2, 2 * K, K), (2 * K) ** -0.5, 0.25, (), jnp.float32)
    phase = jnp.clip(jax.random.uniform(key_list[6], (N_BOX, N_PARAM, LEVELS, PAIRS_DEV, K), jnp.float32, -3.140625, 3.140625), -3.140625, 3.140625)
    return {"traces": traces, "owners": owners, "counts": counts, "pair_table": pair_table, "anterp": anterp, "interp": interp, "phase": phase}


HIGH = lax.Precision.HIGHEST


def rotate(weights_now, angles):
    cosine = jnp.cos(angles)
    sine_part = jnp.sin(angles)
    real_part = weights_now[..., 0, :, :]
    imag_part = weights_now[..., 1, :, :]
    return jnp.stack([real_part * cosine - imag_part * sine_part, real_part * sine_part + imag_part * cosine], axis=-3)


def reference(traces, owners, counts, pair_table, anterp, interp, phase):
    row_ids = jnp.arange(BLK_DEV, dtype=jnp.int32)
    live_mask = (row_ids[None, None, :] < counts[:, :, None]).astype(jnp.float32)
    destination = owners[..., 0]
    onehot = (destination[..., None] == jnp.arange(N_PARAM, dtype=jnp.int32)).astype(jnp.int32)
    ranking = jnp.sum((jnp.cumsum(onehot, axis=2) - onehot) * onehot, axis=-1).astype(jnp.int32)
    box_ids = jnp.arange(N_BOX, dtype=jnp.int32)[:, None, None]
    source_ids = jnp.arange(N_PARAM, dtype=jnp.int32)[None, :, None]
    pair_ids = pair_table[box_ids, destination, source_ids, ranking]
    coefficient = jnp.einsum("bpnt,tk->bpnk", traces * live_mask[..., None], anterp, precision=HIGH)
    target = ((box_ids * N_PARAM + destination) * PAIRS_DEV + pair_ids).astype(jnp.int32)
    summed = jax.ops.segment_sum(coefficient.reshape(-1, 2 * K), target.reshape(-1), num_segments=N_BOX * N_PARAM * PAIRS_DEV)
    summed = summed.reshape(N_BOX, N_PARAM, PAIRS_DEV, 2, K)
    weights_now = jnp.transpose(summed, (0, 1, 3, 2, 4))
    half_rows = PAIRS_DEV // 2
    for level_id in range(LEVELS):
        span_size = 2 ** level_id
        outer_count = N_BOX // (2 * span_size)
        grouped = weights_now.reshape(outer_count, 2, span_size, N_PARAM, 2, 2, half_rows, K)
        side_parts = []
        for side_id in range(2):
            joined = jnp.concatenate([grouped[:, 0, :, :, :, side_id], grouped[:, 1, :, :, :, side_id]], axis=-1)
            combined = jnp.einsum("hlprqk,skj->hlprsqj", joined, interp, precision=HIGH)
            side_parts.append(combined.reshape(outer_count, span_size, N_PARAM, 2, PAIRS_DEV, K))
        weights_now = jnp.stack(side_parts, axis=1).reshape(N_BOX, N_PARAM, 2, PAIRS_DEV, K)
        weights_now = rotate(weights_now, phase[:, :, level_id])
    return weights_now
```

```python
import functools

import jax
import jax.numpy as jnp
from jax import lax
from jax.experimental import pallas as pl
from jax.experimental.pallas import tpu as pltpu
from jax.sharding import PartitionSpec as P

LEVELS = 3
CHUNKS = 4
MESH = pl.DeviceIdType.MESH
F32 = jnp.float32
BF16 = jnp.bfloat16

SIN_TERMS = (-1 / 6, 1 / 120, -1 / 5040, 1 / 362880, -1 / 39916800)
COS_TERMS = (-1 / 2, 1 / 24, -1 / 720, 1 / 40320, -1 / 3628800, 1 / 479001600)


def split(x):
    high = x.astype(BF16)
    return high, (x - high.astype(F32)).astype(BF16)


def dot(a, b):
    return jnp.dot(a, b, preferred_element_type=F32)


def dot3(a, b):
    return dot(a[0], b[0]) + (dot(a[0], b[1]) + dot(a[1], b[0]))


def flag(condition):
    return jnp.where(condition, 1.0, 0.0).astype(BF16)


def flipped(index, mask):
    out = index
    bit = 1
    while bit <= mask:
        if mask & bit:
            out = out + bit * (1 - 2 * ((index // bit) % 2))
        bit *= 2
    return out


def sin_cos(x):
    h = x * 0.5
    y = h * h
    s = jnp.full_like(y, SIN_TERMS[-1])
    for term in SIN_TERMS[-2::-1]:
        s = s * y + term
    s = h + h * (y * s)
    c = jnp.full_like(y, COS_TERMS[-1])
    for term in COS_TERMS[-2::-1]:
        c = c * y + term
    c = 1.0 + y * c
    return 2.0 * s * c, 1.0 - 2.0 * s * s


def kernel(
    param_count,
    traces,
    owners,
    counts,
    pairs,
    anterp,
    interp,
    phase,
    out,
    going,
    arrived,
    selector,
    first_map,
    level_map,
    cosines,
    sines,
    send0,
    recv0,
    kept0,
    send,
    recv,
    kept,
    gather_send,
    gather_recv,
    level_send,
    level_recv,
):
    box = lax.axis_index("box")
    me = lax.axis_index("param")
    rows_total, samples = traces.shape
    slots = pairs.shape[1]
    weights = interp.shape[2]
    half = phase.shape[1] // 2
    rows = half // CHUNKS
    bits = [(box // 2**level) % 2 for level in range(LEVELS)]
    partners = [flipped(box, 2**level) for level in range(LEVELS)]
    peers = [flipped(me, j) for j in range(param_count)]

    barrier = pltpu.get_barrier_semaphore()
    for j in range(1, param_count):
        pl.semaphore_signal(barrier, inc=1, device_id=(box, peers[j]), device_id_type=MESH)
    for level in range(LEVELS):
        pl.semaphore_signal(barrier, inc=1, device_id=(partners[level], me), device_id_type=MESH)

    owner = owners[...]
    owner_rows = max(param_count, 16)
    named = owner == lax.broadcasted_iota(jnp.int32, (owner_rows, rows_total), 0)
    before = flag(
        lax.broadcasted_iota(jnp.int32, (rows_total, rows_total), 0)
        < lax.broadcasted_iota(jnp.int32, (rows_total, rows_total), 1)
    )
    running = dot(flag(named), before)
    rank = jnp.sum(jnp.where(named, running, 0.0), axis=0, keepdims=True).astype(jnp.int32)
    live = lax.broadcasted_iota(jnp.int32, (1, rows_total), 1) < counts[0, 0]
    masked = split(traces[...])
    slot_ids = lax.broadcasted_iota(jnp.int32, (slots, rows_total), 0)

    def block_for(target):
        key = jnp.where((owner == target) & live, rank, -1)
        chosen = flag(slot_ids == key)
        return dot(chosen, masked[0]) + dot(chosen, masked[1])

    pl.semaphore_wait(barrier, param_count - 1 + LEVELS)
    gathers = []
    for j in range(param_count - 1, 0, -1):
        going[j - 1] = block_for(peers[j])
        copy = pltpu.make_async_remote_copy(
            src_ref=going.at[j - 1],
            dst_ref=arrived.at[j - 1],
            send_sem=gather_send.at[j - 1],
            recv_sem=gather_recv.at[j - 1],
            device_id=(box, peers[j]),
            device_id_type=MESH,
        )
        copy.start()
        gathers.append((j, copy))
    own_block = split(block_for(me))

    pair_ids = lax.broadcasted_iota(jnp.int32, (half, slots), 0)
    for j in range(param_count):
        table = pairs[pl.ds(peers[j], 1), :]
        selector[j, 0] = flag(pair_ids + (1 - bits[0]) * half == table)
        selector[j, 1] = flag(pair_ids + bits[0] * half == table)

    for side in range(2):
        for s in range(2):
            piece = split(interp[s, side * weights : (side + 1) * weights, :])
            level_map[0, side, s] = piece[0]
            level_map[1, side, s] = piece[1]
            for r in range(2):
                product = dot3(split(anterp[:, r * weights : (r + 1) * weights]), piece)
                high, low = split(product)
                first_map[0, side, s, :, r * weights : (r + 1) * weights] = high
                first_map[1, side, s, :, r * weights : (r + 1) * weights] = low

    for level in range(LEVELS):
        def angles(step, carry):
            at = pl.ds(pl.multiple_of(step * 16, 16), 16)
            sine, cosine = sin_cos(phase[level, at, :])
            sines[level, at, :] = sine
            cosines[level, at, :] = cosine
            return carry

        lax.fori_loop(0, 2 * half // 16, angles, 0, unroll=2)

    blocks = [(0, own_block)]
    for j, copy in gathers[::-1]:
        copy.wait_recv()
        blocks.append((j, split(arrived[j - 1])))

    def summed(which):
        total = None
        for j, (high, low) in blocks:
            chosen = selector[j, which]
            part = dot(chosen, high) + dot(chosen, low)
            total = part if total is None else total + part
        return total

    def exchange(level, i, source, target):
        copy = pltpu.make_async_remote_copy(
            src_ref=source,
            dst_ref=target,
            send_sem=level_send.at[level, i],
            recv_sem=level_recv.at[level, i],
            device_id=(partners[level], me),
            device_id_type=MESH,
        )
        copy.start()
        return copy

    copies = {}
    send0[...] = summed(0)
    for i in range(CHUNKS):
        at = pl.ds(i * rows, rows)
        copies[0, i] = exchange(0, i, send0.at[at], recv0.at[at])
    kept0[...] = summed(1)

    def turned(level, s, i, real, imag):
        at = pl.ds(pl.multiple_of(s * half + i * rows, rows), rows)
        cosine = cosines[level, at, :]
        sine = sines[level, at, :]
        return real * cosine - imag * sine, real * sine + imag * cosine

    def combined(level, i, s, mine, other):
        side = bits[level]
        if level == 0:
            both = dot3(mine, (first_map[0, side, s], first_map[1, side, s])) + dot3(
                other, (first_map[0, 1 - side, s], first_map[1, 1 - side, s])
            )
            real, imag = both[:, :weights], both[:, weights:]
        else:
            both = dot3(mine, (level_map[0, side, s], level_map[1, side, s])) + dot3(
                other, (level_map[0, 1 - side, s], level_map[1, 1 - side, s])
            )
            real, imag = both[:rows], both[rows:]
        return turned(level, s, i, real, imag)

    def step(level, i):
        copies[level, i].wait_recv()
        if level == 0:
            at = pl.ds(i * rows, rows)
            mine, other = split(kept0[at, :]), split(recv0[at, :])
        else:
            mine = split(kept[level - 1, i].reshape(2 * rows, weights))
            other = split(recv[level - 1, i].reshape(2 * rows, weights))
        if level < LEVELS - 1:
            bit = bits[level + 1]
            real, imag = combined(level, i, 1 - bit, mine, other)
            send[level, i, 0] = real
            send[level, i, 1] = imag
            copies[level + 1, i] = exchange(
                level + 1, i, send.at[level, i], recv.at[level, i]
            )
            real, imag = combined(level, i, bit, mine, other)
            kept[level, i, 0] = real
            kept[level, i, 1] = imag
        else:
            for s in range(2):
                real, imag = combined(level, i, s, mine, other)
                out[0, s * half + i * rows : s * half + (i + 1) * rows, :] = real
                out[1, s * half + i * rows : s * half + (i + 1) * rows, :] = imag

    for t in range(CHUNKS + 1):
        if t < CHUNKS:
            step(0, t)
        if t >= 1:
            step(1, t - 1)
    for i in range(CHUNKS):
        step(2, i)

    for _, copy in gathers:
        copy.wait_send()
    for copy in copies.values():
        copy.wait_send()


def shards(param_count, traces, owners, counts, pair_table, anterp, interp, phase):
    rows_total, samples = traces.shape[2:]
    slots = pair_table.shape[3]
    pair_count, weights = phase.shape[3:]
    half = pair_count // 2
    rows = half // CHUNKS
    vmem = pl.BlockSpec(memory_space=pltpu.VMEM)
    smem = pl.BlockSpec(memory_space=pltpu.SMEM)
    others = param_count - 1
    result = pl.pallas_call(
        functools.partial(kernel, param_count),
        out_shape=jax.ShapeDtypeStruct((2, pair_count, weights), F32),
        in_specs=[vmem, vmem, smem, vmem, vmem, vmem, vmem],
        out_specs=vmem,
        scratch_shapes=[
            pltpu.VMEM((others, slots, samples), F32),
            pltpu.VMEM((others, slots, samples), F32),
            pltpu.VMEM((param_count, 2, half, slots), BF16),
            pltpu.VMEM((2, 2, 2, samples, 2 * weights), BF16),
            pltpu.VMEM((2, 2, 2, weights, weights), BF16),
            pltpu.VMEM((LEVELS, pair_count, weights), F32),
            pltpu.VMEM((LEVELS, pair_count, weights), F32),
            pltpu.VMEM((half, samples), F32),
            pltpu.VMEM((half, samples), F32),
            pltpu.VMEM((half, samples), F32),
            pltpu.VMEM((LEVELS - 1, CHUNKS, 2, rows, weights), F32),
            pltpu.VMEM((LEVELS - 1, CHUNKS, 2, rows, weights), F32),
            pltpu.VMEM((LEVELS - 1, CHUNKS, 2, rows, weights), F32),
            pltpu.SemaphoreType.DMA((others,)),
            pltpu.SemaphoreType.DMA((others,)),
            pltpu.SemaphoreType.DMA((LEVELS, CHUNKS)),
            pltpu.SemaphoreType.DMA((LEVELS, CHUNKS)),
        ],
        compiler_params=pltpu.CompilerParams(
            collective_id=0, has_side_effects=True, vmem_limit_bytes=50 * 2**20
        ),
    )(
        traces[0, 0],
        owners.reshape(1, rows_total),
        counts,
        pair_table[0, 0],
        anterp,
        interp,
        phase[0, 0],
    )
    return result[None, None]


def solution(mesh):
    placed = (
        P("box", "param", None, None),
        P("box", "param", None, None),
        P("box", "param"),
        P("box", "param", None, None),
        P(),
        P(),
        P("box", "param", None, None, None),
    )
    return jax.shard_map(
        functools.partial(shards, mesh.shape["param"]),
        mesh=mesh,
        in_specs=placed,
        out_specs=P("box", "param", None, None, None),
        check_vma=False,
    )
```

```python
import functools

import jax
import jax.numpy as jnp
from jax import lax
from jax.experimental import pallas as pl
from jax.experimental.pallas import tpu as pltpu
from jax.sharding import PartitionSpec as P

LEVELS = 3
CHUNKS = 8
LAG = 1
MESH = pl.DeviceIdType.MESH
F32 = jnp.float32
BF16 = jnp.bfloat16

SIN_TERMS = (-1 / 6, 1 / 120, -1 / 5040, 1 / 362880, -1 / 39916800)
COS_TERMS = (-1 / 2, 1 / 24, -1 / 720, 1 / 40320, -1 / 3628800, 1 / 479001600)


def split(x):
    high = x.astype(BF16)
    return high, (x - high.astype(F32)).astype(BF16)


def dot(a, b):
    return jnp.dot(a, b, preferred_element_type=F32)


def dot3(a, b):
    return dot(a[0], b[0]) + (dot(a[0], b[1]) + dot(a[1], b[0]))


def flag(condition):
    return jnp.where(condition, 1.0, 0.0).astype(BF16)


def flipped(index, mask):
    out = index
    bit = 1
    while bit <= mask:
        if mask & bit:
            out = out + bit * (1 - 2 * ((index // bit) % 2))
        bit *= 2
    return out


def sin_cos(x):
    h = x * 0.5
    y = h * h
    s = jnp.full_like(y, SIN_TERMS[-1])
    for term in SIN_TERMS[-2::-1]:
        s = s * y + term
    s = h + h * (y * s)
    c = jnp.full_like(y, COS_TERMS[-1])
    for term in COS_TERMS[-2::-1]:
        c = c * y + term
    c = 1.0 + y * c
    return 2.0 * s * c, 1.0 - 2.0 * s * s


def kernel(
    param_count,
    traces_hbm,
    owners,
    counts,
    pairs,
    anterp_hbm,
    interp_hbm,
    phase_hbm,
    out_hbm,
    out,
    traces,
    anterp,
    interp,
    phase,
    going,
    arrived,
    selector,
    first_map,
    level_map,
    cosines,
    sines,
    send0,
    recv0,
    kept0,
    send,
    recv,
    kept,
    load_sem,
    store_sem,
    gather_send,
    gather_recv,
    level_send,
    level_recv,
):
    loads = [
        pltpu.make_async_copy(source, target, load_sem.at[k])
        for k, (source, target) in enumerate(
            [
                (traces_hbm, traces),
                (anterp_hbm, anterp),
                (interp_hbm, interp),
                (phase_hbm, phase),
            ]
        )
    ]
    for load in loads:
        load.start()

    box = lax.axis_index("box")
    me = lax.axis_index("param")
    rows_total, samples = traces.shape
    slots = pairs.shape[1]
    weights = interp.shape[2]
    half = phase.shape[1] // 2
    rows = half // CHUNKS
    bits = [(box // 2**level) % 2 for level in range(LEVELS)]
    partners = [flipped(box, 2**level) for level in range(LEVELS)]
    peers = [flipped(me, j) for j in range(param_count)]

    barrier = pltpu.get_barrier_semaphore()
    for j in range(1, param_count):
        pl.semaphore_signal(barrier, inc=1, device_id=(box, peers[j]), device_id_type=MESH)
    for level in range(LEVELS):
        pl.semaphore_signal(barrier, inc=1, device_id=(partners[level], me), device_id_type=MESH)

    owner = owners[...]
    owner_rows = max(param_count, 16)
    named = owner == lax.broadcasted_iota(jnp.int32, (owner_rows, rows_total), 0)
    before = flag(
        lax.broadcasted_iota(jnp.int32, (rows_total, rows_total), 0)
        < lax.broadcasted_iota(jnp.int32, (rows_total, rows_total), 1)
    )
    running = dot(flag(named), before)
    rank = jnp.sum(jnp.where(named, running, 0.0), axis=0, keepdims=True).astype(jnp.int32)
    live = lax.broadcasted_iota(jnp.int32, (1, rows_total), 1) < counts[0, 0]
    loads[0].wait()
    masked = split(traces[...])
    slot_ids = lax.broadcasted_iota(jnp.int32, (slots, rows_total), 0)

    def block_for(target):
        key = jnp.where((owner == target) & live, rank, -1)
        chosen = flag(slot_ids == key)
        return dot(chosen, masked[0]) + dot(chosen, masked[1])

    pl.semaphore_wait(barrier, param_count - 1 + LEVELS)
    gathers = []
    for j in range(param_count - 1, 0, -1):
        going[j - 1] = block_for(peers[j])
        copy = pltpu.make_async_remote_copy(
            src_ref=going.at[j - 1],
            dst_ref=arrived.at[j - 1],
            send_sem=gather_send.at[j - 1],
            recv_sem=gather_recv.at[j - 1],
            device_id=(box, peers[j]),
            device_id_type=MESH,
        )
        copy.start()
        gathers.append((j, copy))
    own_block = split(block_for(me))

    pair_ids = lax.broadcasted_iota(jnp.int32, (half, slots), 0)
    for j in range(param_count):
        table = pairs[pl.ds(peers[j], 1), :]
        selector[j, 0] = flag(pair_ids + (1 - bits[0]) * half == table)
        selector[j, 1] = flag(pair_ids + bits[0] * half == table)

    loads[1].wait()
    loads[2].wait()
    for side in range(2):
        for s in range(2):
            piece = split(interp[s, side * weights : (side + 1) * weights, :])
            level_map[0, side, s] = piece[0]
            level_map[1, side, s] = piece[1]
            for r in range(2):
                product = dot3(split(anterp[:, r * weights : (r + 1) * weights]), piece)
                high, low = split(product)
                first_map[0, side, s, :, r * weights : (r + 1) * weights] = high
                first_map[1, side, s, :, r * weights : (r + 1) * weights] = low

    loads[3].wait()
    for level in range(LEVELS):
        def angles(step, carry):
            at = pl.ds(pl.multiple_of(step * 16, 16), 16)
            sine, cosine = sin_cos(phase[level, at, :])
            sines[level, at, :] = sine
            cosines[level, at, :] = cosine
            return carry

        lax.fori_loop(0, 2 * half // 16, angles, 0, unroll=2)

    def part(j, which, at, values):
        chosen = selector[j, which, at, :]
        return dot(chosen, values[0]) + dot(chosen, values[1])

    every = pl.ds(0, half)
    send0[...] = part(0, 0, every, own_block)
    kept0[...] = part(0, 1, every, own_block)
    blocks = []
    for j, copy in gathers[::-1]:
        copy.wait_recv()
        block = split(arrived[j - 1])
        if j == 1:
            send0[...] += part(j, 0, every, block)
            kept0[...] += part(j, 1, every, block)
        else:
            blocks.append((j, block))

    def exchange(level, i, source, target):
        copy = pltpu.make_async_remote_copy(
            src_ref=source,
            dst_ref=target,
            send_sem=level_send.at[level, i],
            recv_sem=level_recv.at[level, i],
            device_id=(partners[level], me),
            device_id_type=MESH,
        )
        copy.start()
        return copy

    copies = {}
    stores = []
    for i in range(CHUNKS):
        at = pl.ds(i * rows, rows)
        for j, block in blocks:
            send0[at, :] += part(j, 0, at, block)
        copies[0, i] = exchange(0, i, send0.at[at], recv0.at[at])
    for j, block in blocks:
        kept0[...] += part(j, 1, every, block)

    def turned(level, s, i, real, imag):
        at = pl.ds(pl.multiple_of(s * half + i * rows, rows), rows)
        cosine = cosines[level, at, :]
        sine = sines[level, at, :]
        return real * cosine - imag * sine, real * sine + imag * cosine

    def combined(level, i, s, mine, other):
        side = bits[level]
        if level == 0:
            both = dot3(mine, (first_map[0, side, s], first_map[1, side, s])) + dot3(
                other, (first_map[0, 1 - side, s], first_map[1, 1 - side, s])
            )
            real, imag = both[:, :weights], both[:, weights:]
        else:
            both = dot3(mine, (level_map[0, side, s], level_map[1, side, s])) + dot3(
                other, (level_map[0, 1 - side, s], level_map[1, 1 - side, s])
            )
            real, imag = both[:rows], both[rows:]
        return turned(level, s, i, real, imag)

    def step(level, i):
        copies[level, i].wait_recv()
        if level == 0:
            at = pl.ds(i * rows, rows)
            mine, other = split(kept0[at, :]), split(recv0[at, :])
        else:
            mine = split(kept[level - 1, i].reshape(2 * rows, weights))
            other = split(recv[level - 1, i].reshape(2 * rows, weights))
        if level < LEVELS - 1:
            bit = bits[level + 1]
            real, imag = combined(level, i, 1 - bit, mine, other)
            send[level, i, 0] = real
            send[level, i, 1] = imag
            copies[level + 1, i] = exchange(
                level + 1, i, send.at[level, i], recv.at[level, i]
            )
            real, imag = combined(level, i, bit, mine, other)
            kept[level, i, 0] = real
            kept[level, i, 1] = imag
        else:
            for s in range(2):
                real, imag = combined(level, i, s, mine, other)
                at = pl.ds(s * half + i * rows, rows)
                out[0, at, :] = real
                out[1, at, :] = imag
                for r in range(2):
                    store = pltpu.make_async_copy(
                        out.at[r, at], out_hbm.at[r, at], store_sem.at[i, s, r]
                    )
                    store.start()
                    stores.append(store)

    for t in range(CHUNKS + LAG):
        if t < CHUNKS:
            step(0, t)
        if t >= LAG:
            step(1, t - LAG)
    for i in range(CHUNKS):
        step(2, i)

    for store in stores:
        store.wait()
    for _, copy in gathers:
        copy.wait_send()
    for copy in copies.values():
        copy.wait_send()


def shards(param_count, traces, owners, counts, pair_table, anterp, interp, phase):
    rows_total, samples = traces.shape[2:]
    slots = pair_table.shape[3]
    pair_count, weights = phase.shape[3:]
    half = pair_count // 2
    rows = half // CHUNKS
    vmem = pl.BlockSpec(memory_space=pltpu.VMEM)
    smem = pl.BlockSpec(memory_space=pltpu.SMEM)
    hbm = pl.BlockSpec(memory_space=pltpu.HBM)
    others = param_count - 1
    result = pl.pallas_call(
        functools.partial(kernel, param_count),
        out_shape=jax.ShapeDtypeStruct((2, pair_count, weights), F32),
        in_specs=[hbm, vmem, smem, vmem, hbm, hbm, hbm],
        out_specs=hbm,
        scratch_shapes=[
            pltpu.VMEM((2, pair_count, weights), F32),
            pltpu.VMEM((rows_total, samples), F32),
            pltpu.VMEM(anterp.shape, F32),
            pltpu.VMEM(interp.shape, F32),
            pltpu.VMEM((LEVELS, pair_count, weights), F32),
            pltpu.VMEM((others, slots, samples), F32),
            pltpu.VMEM((others, slots, samples), F32),
            pltpu.VMEM((param_count, 2, half, slots), BF16),
            pltpu.VMEM((2, 2, 2, samples, 2 * weights), BF16),
            pltpu.VMEM((2, 2, 2, weights, weights), BF16),
            pltpu.VMEM((LEVELS, pair_count, weights), F32),
            pltpu.VMEM((LEVELS, pair_count, weights), F32),
            pltpu.VMEM((half, samples), F32),
            pltpu.VMEM((half, samples), F32),
            pltpu.VMEM((half, samples), F32),
            pltpu.VMEM((LEVELS - 1, CHUNKS, 2, rows, weights), F32),
            pltpu.VMEM((LEVELS - 1, CHUNKS, 2, rows, weights), F32),
            pltpu.VMEM((LEVELS - 1, CHUNKS, 2, rows, weights), F32),
            pltpu.SemaphoreType.DMA((4,)),
            pltpu.SemaphoreType.DMA((CHUNKS, 2, 2)),
            pltpu.SemaphoreType.DMA((others,)),
            pltpu.SemaphoreType.DMA((others,)),
            pltpu.SemaphoreType.DMA((LEVELS, CHUNKS)),
            pltpu.SemaphoreType.DMA((LEVELS, CHUNKS)),
        ],
        compiler_params=pltpu.CompilerParams(
            collective_id=0, has_side_effects=True, vmem_limit_bytes=60 * 2**20
        ),
    )(
        traces[0, 0],
        owners.reshape(1, rows_total),
        counts,
        pair_table[0, 0],
        anterp,
        interp,
        phase[0, 0],
    )
    return result[None, None]


def solution(mesh):
    placed = (
        P("box", "param", None, None),
        P("box", "param", None, None),
        P("box", "param"),
        P("box", "param", None, None),
        P(),
        P(),
        P("box", "param", None, None, None),
    )
    return jax.shard_map(
        functools.partial(shards, mesh.shape["param"]),
        mesh=mesh,
        in_specs=placed,
        out_specs=P("box", "param", None, None, None),
        check_vma=False,
    )
```

```python
import functools

import jax
import jax.numpy as jnp
from jax import lax
from jax.experimental import pallas as pl
from jax.experimental.pallas import tpu as pltpu
from jax.sharding import PartitionSpec as P

LEVELS = 3
CHUNKS = 8
LAG = 1
MESH = pl.DeviceIdType.MESH
F32 = jnp.float32
BF16 = jnp.bfloat16

SIN_TERMS = (-1 / 6, 1 / 120, -1 / 5040, 1 / 362880, -1 / 39916800)
COS_TERMS = (-1 / 2, 1 / 24, -1 / 720, 1 / 40320, -1 / 3628800, 1 / 479001600)


def split(x):
    high = x.astype(BF16)
    return high, (x - high.astype(F32)).astype(BF16)


def dot(a, b):
    return jnp.dot(a, b, preferred_element_type=F32)


def dot3(a, b):
    return dot(a[0], b[0]) + (dot(a[0], b[1]) + dot(a[1], b[0]))


def flag(condition):
    return jnp.where(condition, 1.0, 0.0).astype(BF16)


def flipped(index, mask):
    out = index
    bit = 1
    while bit <= mask:
        if mask & bit:
            out = out + bit * (1 - 2 * ((index // bit) % 2))
        bit *= 2
    return out


def sin_cos(x):
    h = x * 0.5
    y = h * h
    s = jnp.full_like(y, SIN_TERMS[-1])
    for term in SIN_TERMS[-2::-1]:
        s = s * y + term
    s = h + h * (y * s)
    c = jnp.full_like(y, COS_TERMS[-1])
    for term in COS_TERMS[-2::-1]:
        c = c * y + term
    c = 1.0 + y * c
    return 2.0 * s * c, 1.0 - 2.0 * s * s


def kernel(
    param_count,
    traces_hbm,
    owners,
    counts,
    pairs,
    anterp_hbm,
    interp_hbm,
    phase_hbm,
    out_hbm,
    out,
    traces,
    anterp,
    interp,
    phase,
    going,
    arrived,
    selector,
    first_map,
    level_map,
    cosines,
    sines,
    send0,
    recv0,
    kept0,
    send,
    recv,
    kept,
    load_sem,
    store_sem,
    gather_send,
    gather_recv,
    level_send,
    level_recv,
):
    loads = [
        pltpu.make_async_copy(source, target, load_sem.at[k])
        for k, (source, target) in enumerate(
            [
                (traces_hbm, traces),
                (anterp_hbm, anterp),
                (interp_hbm, interp),
                (phase_hbm, phase),
            ]
        )
    ]
    for load in loads:
        load.start()

    box = lax.axis_index("box")
    me = lax.axis_index("param")
    rows_total, samples = traces.shape
    slots = pairs.shape[1]
    weights = interp.shape[2]
    half = phase.shape[1] // 2
    rows = half // CHUNKS
    bits = [(box // 2**level) % 2 for level in range(LEVELS)]
    partners = [flipped(box, 2**level) for level in range(LEVELS)]
    peers = [flipped(me, j) for j in range(param_count)]

    barrier = pltpu.get_barrier_semaphore()
    for j in range(1, param_count):
        pl.semaphore_signal(barrier, inc=1, device_id=(box, peers[j]), device_id_type=MESH)
    for level in range(LEVELS):
        pl.semaphore_signal(barrier, inc=1, device_id=(partners[level], me), device_id_type=MESH)

    owner = owners[...]
    owner_rows = max(param_count, 16)
    named = owner == lax.broadcasted_iota(jnp.int32, (owner_rows, rows_total), 0)
    before = flag(
        lax.broadcasted_iota(jnp.int32, (rows_total, rows_total), 0)
        < lax.broadcasted_iota(jnp.int32, (rows_total, rows_total), 1)
    )
    running = dot(flag(named), before)
    rank = jnp.sum(jnp.where(named, running, 0.0), axis=0, keepdims=True).astype(jnp.int32)
    live = lax.broadcasted_iota(jnp.int32, (1, rows_total), 1) < counts[0, 0]
    loads[0].wait()
    masked = split(traces[...])
    slot_ids = lax.broadcasted_iota(jnp.int32, (slots, rows_total), 0)

    def block_for(target):
        key = jnp.where((owner == target) & live, rank, -1)
        chosen = flag(slot_ids == key)
        return dot(chosen, masked[0]) + dot(chosen, masked[1])

    pl.semaphore_wait(barrier, param_count - 1 + LEVELS)
    gathers = []
    for j in range(param_count - 1, 0, -1):
        going[j - 1] = block_for(peers[j])
        copy = pltpu.make_async_remote_copy(
            src_ref=going.at[j - 1],
            dst_ref=arrived.at[j - 1],
            send_sem=gather_send.at[j - 1],
            recv_sem=gather_recv.at[j - 1],
            device_id=(box, peers[j]),
            device_id_type=MESH,
        )
        copy.start()
        gathers.append((j, copy))
    own_block = split(block_for(me))

    pair_ids = lax.broadcasted_iota(jnp.int32, (half, slots), 0)
    for j in range(param_count):
        table = pairs[pl.ds(peers[j], 1), :]
        selector[j, 0] = flag(pair_ids + (1 - bits[0]) * half == table)
        selector[j, 1] = flag(pair_ids + bits[0] * half == table)

    loads[1].wait()
    loads[2].wait()
    for side in range(2):
        for s in range(2):
            piece = split(interp[s, side * weights : (side + 1) * weights, :])
            level_map[0, side, s] = piece[0]
            level_map[1, side, s] = piece[1]
            for r in range(2):
                product = dot3(split(anterp[:, r * weights : (r + 1) * weights]), piece)
                high, low = split(product)
                first_map[0, side, s, :, r * weights : (r + 1) * weights] = high
                first_map[1, side, s, :, r * weights : (r + 1) * weights] = low

    loads[3].wait()
    for level in range(LEVELS):
        def angles(step, carry):
            at = pl.ds(pl.multiple_of(step * 16, 16), 16)
            sine, cosine = sin_cos(phase[level, at, :])
            sines[level, at, :] = sine
            cosines[level, at, :] = cosine
            return carry

        lax.fori_loop(0, 2 * half // 16, angles, 0, unroll=2)

    def part(j, which, at, values):
        chosen = selector[j, which, at, :]
        return dot(chosen, values[0]) + dot(chosen, values[1])

    every = pl.ds(0, half)
    send0[...] = part(0, 0, every, own_block)
    kept0[...] = part(0, 1, every, own_block)
    blocks = []
    for j, copy in gathers[::-1]:
        copy.wait_recv()
        block = split(arrived[j - 1])
        if j == 1:
            send0[...] += part(j, 0, every, block)
            kept0[...] += part(j, 1, every, block)
        else:
            blocks.append((j, block))

    def exchange(level, i, source, target):
        copy = pltpu.make_async_remote_copy(
            src_ref=source,
            dst_ref=target,
            send_sem=level_send.at[level, i],
            recv_sem=level_recv.at[level, i],
            device_id=(partners[level], me),
            device_id_type=MESH,
        )
        copy.start()
        return copy

    copies = {}
    stores = []
    for i in range(CHUNKS):
        at = pl.ds(i * rows, rows)
        for j, block in blocks:
            send0[at, :] += part(j, 0, at, block)
        copies[0, i] = exchange(0, i, send0.at[at], recv0.at[at])
    for j, block in blocks:
        kept0[...] += part(j, 1, every, block)

    def turned(level, s, i, real, imag):
        at = pl.ds(pl.multiple_of(s * half + i * rows, rows), rows)
        cosine = cosines[level, at, :]
        sine = sines[level, at, :]
        return real * cosine - imag * sine, real * sine + imag * cosine

    def combined(level, i, s, mine, other):
        side = bits[level]
        if level == 0:
            both = dot3(mine, (first_map[0, side, s], first_map[1, side, s])) + dot3(
                other, (first_map[0, 1 - side, s], first_map[1, 1 - side, s])
            )
            real, imag = both[:, :weights], both[:, weights:]
        else:
            both = dot3(mine, (level_map[0, side, s], level_map[1, side, s])) + dot3(
                other, (level_map[0, 1 - side, s], level_map[1, 1 - side, s])
            )
            real, imag = both[:rows], both[rows:]
        return turned(level, s, i, real, imag)

    def keep(level, i, mine, other):
        real, imag = combined(level, i, bits[level + 1], mine, other)
        kept[level, i, 0] = real
        kept[level, i, 1] = imag

    def operands(level, i):
        return (
            split(kept[level - 1, i].reshape(2 * rows, weights)),
            split(recv[level - 1, i].reshape(2 * rows, weights)),
        )

    def step(level, i):
        copies[level, i].wait_recv()
        if level == 0:
            at = pl.ds(i * rows, rows)
            mine, other = split(kept0[at, :]), split(recv0[at, :])
        else:
            mine = split(kept[level - 1, i].reshape(2 * rows, weights))
            other = split(recv[level - 1, i].reshape(2 * rows, weights))
        if level < LEVELS - 1:
            bit = bits[level + 1]
            real, imag = combined(level, i, 1 - bit, mine, other)
            send[level, i, 0] = real
            send[level, i, 1] = imag
            copies[level + 1, i] = exchange(
                level + 1, i, send.at[level, i], recv.at[level, i]
            )
            if level == 0:
                keep(level, i, mine, other)
        else:
            for s in range(2):
                real, imag = combined(level, i, s, mine, other)
                at = pl.ds(s * half + i * rows, rows)
                out[0, at, :] = real
                out[1, at, :] = imag
                for r in range(2):
                    store = pltpu.make_async_copy(
                        out.at[r, at], out_hbm.at[r, at], store_sem.at[i, s, r]
                    )
                    store.start()
                    stores.append(store)

    for t in range(CHUNKS + LAG):
        if t < CHUNKS:
            step(0, t)
        if t >= LAG:
            step(1, t - LAG)
    for i in range(CHUNKS):
        keep(1, i, *operands(1, i))
    for i in range(CHUNKS):
        step(2, i)

    for store in stores:
        store.wait()
    for _, copy in gathers:
        copy.wait_send()
    for copy in copies.values():
        copy.wait_send()


def shards(param_count, traces, owners, counts, pair_table, anterp, interp, phase):
    rows_total, samples = traces.shape[2:]
    slots = pair_table.shape[3]
    pair_count, weights = phase.shape[3:]
    half = pair_count // 2
    rows = half // CHUNKS
    vmem = pl.BlockSpec(memory_space=pltpu.VMEM)
    smem = pl.BlockSpec(memory_space=pltpu.SMEM)
    hbm = pl.BlockSpec(memory_space=pltpu.HBM)
    others = param_count - 1
    result = pl.pallas_call(
        functools.partial(kernel, param_count),
        out_shape=jax.ShapeDtypeStruct((2, pair_count, weights), F32),
        in_specs=[hbm, vmem, smem, vmem, hbm, hbm, hbm],
        out_specs=hbm,
        scratch_shapes=[
            pltpu.VMEM((2, pair_count, weights), F32),
            pltpu.VMEM((rows_total, samples), F32),
            pltpu.VMEM(anterp.shape, F32),
            pltpu.VMEM(interp.shape, F32),
            pltpu.VMEM((LEVELS, pair_count, weights), F32),
            pltpu.VMEM((others, slots, samples), F32),
            pltpu.VMEM((others, slots, samples), F32),
            pltpu.VMEM((param_count, 2, half, slots), BF16),
            pltpu.VMEM((2, 2, 2, samples, 2 * weights), BF16),
            pltpu.VMEM((2, 2, 2, weights, weights), BF16),
            pltpu.VMEM((LEVELS, pair_count, weights), F32),
            pltpu.VMEM((LEVELS, pair_count, weights), F32),
            pltpu.VMEM((half, samples), F32),
            pltpu.VMEM((half, samples), F32),
            pltpu.VMEM((half, samples), F32),
            pltpu.VMEM((LEVELS - 1, CHUNKS, 2, rows, weights), F32),
            pltpu.VMEM((LEVELS - 1, CHUNKS, 2, rows, weights), F32),
            pltpu.VMEM((LEVELS - 1, CHUNKS, 2, rows, weights), F32),
            pltpu.SemaphoreType.DMA((4,)),
            pltpu.SemaphoreType.DMA((CHUNKS, 2, 2)),
            pltpu.SemaphoreType.DMA((others,)),
            pltpu.SemaphoreType.DMA((others,)),
            pltpu.SemaphoreType.DMA((LEVELS, CHUNKS)),
            pltpu.SemaphoreType.DMA((LEVELS, CHUNKS)),
        ],
        compiler_params=pltpu.CompilerParams(
            collective_id=0, has_side_effects=True, vmem_limit_bytes=60 * 2**20
        ),
    )(
        traces[0, 0],
        owners.reshape(1, rows_total),
        counts,
        pair_table[0, 0],
        anterp,
        interp,
        phase[0, 0],
    )
    return result[None, None]


def solution(mesh):
    placed = (
        P("box", "param", None, None),
        P("box", "param", None, None),
        P("box", "param"),
        P("box", "param", None, None),
        P(),
        P(),
        P("box", "param", None, None, None),
    )
    return jax.shard_map(
        functools.partial(shards, mesh.shape["param"]),
        mesh=mesh,
        in_specs=placed,
        out_specs=P("box", "param", None, None, None),
        check_vma=False,
    )
```
